256 devices in a mesh: row: 8 (over z_lo, core), col: 32 (over x, z_hi, y).
Axes of the slice: x: 4, y: 4, z: 8 (z_hi: 2, z_lo: 4; z = z_hi * 4 + z_lo), core: 2. Of those that a mesh axis runs over, the one named last changes fastest.
Arguments:
- embedding: bfloat16 [32768, 256], P(('row', 'col')), may hold values from -1.5 to 1.5
- row_blocks: int32 [6144], P(('row', 'col')), may hold values from 0 to 7
- col_blocks: int32 [6144], P(('row', 'col')), may hold values from 0 to 31
- win_counts: bfloat16 [6144, 128, 128], P(('row', 'col')), may hold values from 0 to 2, as said below
- loss_counts: bfloat16 [6144, 128, 128], P(('row', 'col')), may hold values from 0 to 2, as said below
- live_tiles: int32 [256], P(('row', 'col')), may hold values from 1 to 24, as said below
Outputs:
- fitted: float32 [32768, 256], P(('row', 'col'))
The draws below stay inside these ranges and needn't reach their ends.
Inputs may be any that keep to these rules, and one draw needn't show every extreme that they name: `win_counts`: whole numbers. `loss_counts`: whole numbers. `live_tiles`: one device has all 24 slots live.
All inputs are finite; a program needn't handle non-finite values.
Results may differ from the reference program's by a relative error of at most 0.003.
Values may be sent and summed in bfloat16 or wider, within the bound.
No kernel may reach another device: no remote copies, remote signals or barrier semaphores. Data moves between devices by JAX's collectives and lax.ppermute only.
A program may use at most 64 MiB of HBM per device.

```python
import jax
import jax.numpy as jnp
from jax import lax

DIM = 128
TILE = 128
TPD = 24
ITERS = 2
RESP = 32768
SLOTS = 6144
N_ROW = 8
N_COL = 32
DEVICES = 256


def draw_win_counts(key, part):
    key = jax.random.fold_in(key, 11)
    values = jax.random.randint(key, (SLOTS, TILE, TILE), 0, 3, dtype=jnp.int32)
    return values.astype(jnp.bfloat16)


def draw_loss_counts(key, part):
    key = jax.random.fold_in(key, 13)
    values = jax.random.randint(key, (SLOTS, TILE, TILE), 0, 3, dtype=jnp.int32)
    return values.astype(jnp.bfloat16)


def draw_live_tiles(key, part):
    key = jax.random.fold_in(key, 7)
    key_counts, key_pick = jax.random.split(key)
    counts = jax.random.randint(key_counts, (DEVICES,), TPD // 3, TPD // 2 + 1, dtype=jnp.int32)
    chosen = jax.random.randint(key_pick, (), 0, DEVICES, dtype=jnp.int32)
    positions = jnp.arange(DEVICES, dtype=jnp.int32)
    return jnp.where(positions == chosen, TPD, counts).astype(jnp.int32)


def place_ends(values, stream_key, smallest, high):
    extent = values.shape
    index_at = [jax.random.randint(jax.random.fold_in(stream_key, axis), (), 0, extent[axis]) for axis in range(len(extent))]
    values = values.at[tuple(index_at)].set(smallest)
    longest = extent.index(max(extent))
    index_at[longest] = (index_at[longest] + 1) % extent[longest]
    return values.at[tuple(index_at)].set(high)


def levels(stream_key, dims, cuts, smallest, high):
    factor_of, own = 1.0, jax.random.fold_in(stream_key, 6)
    for dim, parts in cuts:
        draws = jnp.exp(jax.random.uniform(jax.random.fold_in(own, dim), (parts,), jnp.float32, smallest / len(cuts), high / len(cuts)))
        factor_of = factor_of * jnp.repeat(draws, dims[dim] // parts).reshape([-1 if axis == dim else 1 for axis in range(len(dims))])
    return factor_of


def gaussian(own_key, shape, deviation, reach, shards=(), kind=jnp.bfloat16):
    factor_of = levels(own_key, shape, shards, -0.22, 0.18) if shards else 1.0
    array = jax.random.normal(own_key, shape, jnp.float32) * deviation * factor_of
    return jnp.minimum(jnp.maximum(array, -reach), reach).astype(kind)


def setup_inputs(seed: int = 0) -> dict:
    splits = jax.random.split(jax.random.key(seed), 7)
    embedding = gaussian(splits[0], (RESP, 2 * DIM), 0.25, 1.5, ((0, 256),))
    row_blocks = place_ends(jax.random.randint(splits[1], (SLOTS,), 0, N_ROW), jax.random.fold_in(splits[1], 1), 0, N_ROW - 1).astype(jnp.int32)
    col_blocks = place_ends(jax.random.randint(splits[2], (SLOTS,), 0, N_COL), jax.random.fold_in(splits[2], 1), 0, N_COL - 1).astype(jnp.int32)
    win_counts = draw_win_counts(jax.random.fold_in(splits[6], 71), 0)
    loss_counts = draw_loss_counts(jax.random.fold_in(splits[6], 71), 0)
    live_tiles = draw_live_tiles(jax.random.fold_in(splits[6], 71), 0)
    return {"embedding": embedding, "row_blocks": row_blocks, "col_blocks": col_blocks, "win_counts": win_counts, "loss_counts": loss_counts, "live_tiles": live_tiles}


def reference(embedding, row_blocks, col_blocks, win_counts, loss_counts, live_tiles):
    half_width = DIM
    slot_ids = jnp.arange(SLOTS, dtype=jnp.int32)
    device_ids = slot_ids // TPD
    row_index = device_ids // N_COL
    col_index = device_ids % N_COL
    first_block = (row_blocks * N_COL + col_index).astype(jnp.int32)
    second_block = (row_index * N_COL + col_blocks).astype(jnp.int32)
    alive = (slot_ids % TPD) < live_tiles[device_ids]
    current = embedding
    result = embedding.astype(jnp.float32)
    for iteration in range(ITERS):
        def visit(grad, inputs):
            first, second, wins, losses, keep = inputs

            def active(grad_in):
                start_one = (first * TILE).astype(jnp.int32)
                start_two = (second * TILE).astype(jnp.int32)
                left_rows = lax.dynamic_slice_in_dim(current, start_one, TILE, 0)
                right_rows = lax.dynamic_slice_in_dim(current, start_two, TILE, 0)
                blade_one, chest_one = left_rows[:, :half_width], left_rows[:, half_width:]
                blade_two, chest_two = right_rows[:, :half_width], right_rows[:, half_width:]
                left_side = jnp.concatenate([blade_one, -chest_one], axis=1)
                right_side = jnp.concatenate([chest_two, blade_two], axis=1)
                score = jnp.dot(left_side, right_side.T, preferred_element_type=jnp.float32)
                wins_f = wins.astype(jnp.float32)
                losses_f = losses.astype(jnp.float32)
                resid = (wins_f - (wins_f + losses_f) * jax.nn.sigmoid(score)).astype(jnp.bfloat16)
                first_grad = jnp.dot(resid, jnp.concatenate([chest_two, -blade_two], axis=1), preferred_element_type=jnp.float32)
                second_grad = jnp.dot(resid.T, jnp.concatenate([-chest_one, blade_one], axis=1), preferred_element_type=jnp.float32)
                block_one = lax.dynamic_slice_in_dim(grad_in, start_one, TILE, 0) + first_grad
                grad_out = lax.dynamic_update_slice_in_dim(grad_in, block_one, start_one, 0)
                block_two = lax.dynamic_slice_in_dim(grad_out, start_two, TILE, 0) + second_grad
                return lax.dynamic_update_slice_in_dim(grad_out, block_two, start_two, 0)

            return lax.cond(keep, active, lambda grad_in: grad_in, grad), None

        grad = jnp.zeros((RESP, 2 * DIM), jnp.float32)
        grad, unused = lax.scan(visit, grad, (first_block, second_block, win_counts, loss_counts, alive))
        result = current.astype(jnp.float32) + 0.01 * grad
        current = result.astype(jnp.bfloat16)
    return result
```

```python
import functools
import itertools

import jax
import jax.numpy as jnp
from jax import lax
from jax.experimental import pallas as pl
from jax.experimental.pallas import tpu as pltpu
from jax.sharding import Mesh
from jax.sharding import PartitionSpec as P

ITERS = 2
RATE = 0.01
GROUP = 4
AXES = ("zl", "core", "x", "zh", "y")
SIZES = (4, 2, 4, 2, 4)


def permutation(move):
    pairs = []
    for source, place in enumerate(itertools.product(*[range(size) for size in SIZES])):
        place = move(dict(zip(AXES, place)))
        target = 0
        for axis, size in zip(AXES, SIZES):
            target = target * size + place[axis] % size
        pairs.append((source, target))
    return pairs


def shift(axis, by):
    def move(place):
        place[axis] += by
        return place

    return permutation(move)


def shift_by_core(axes, by):
    def move(place):
        place[axes[place["core"]]] += by
        return place

    return permutation(move)


def send(values, pairs):
    return lax.ppermute(values, AXES, pairs)


def slot_kernel(
    first_ref, second_ref, live_ref,
    u0, u1, u2, u3, v0, v1, v2, v3, wins, losses,
    near, far, d0, d1, d2, d3,
    left, turned, right, first_sum, second_sum,
):
    half = left.shape[2] // 2
    for index, part in enumerate((u0, u1, u2, u3)):
        for core in range(2):
            block = part[core]
            left[2 * index + core] = block
            turned[2 * index + core, :, :half] = -block[:, half:]
            turned[2 * index + core, :, half:] = block[:, :half]
    for index, part in enumerate((v0, v1, v2, v3)):
        right[pl.ds(8 * index, 8)] = part[...]
    first_sum[...] = jnp.zeros_like(first_sum)
    second_sum[...] = jnp.zeros_like(second_sum)
    live = live_ref[0]

    def step(turn, carry):
        work = []
        for member in range(GROUP):
            slot = turn * GROUP + member
            p, q = first_ref[slot], second_ref[slot]
            score = lax.dot_general(
                turned[p], right[q], (((1,), (1,)), ((), ())), preferred_element_type=jnp.float32
            )
            won = wins[slot].astype(jnp.float32)
            lost = losses[slot].astype(jnp.float32)
            resid = won - (won + lost) * jax.nn.sigmoid(score)
            resid = jnp.where(slot < live, resid, 0.0).astype(jnp.bfloat16)
            work.append((p, q, resid))
        grads = []
        for p, q, resid in work:
            first = jnp.dot(resid, right[q], preferred_element_type=jnp.float32)
            second = lax.dot_general(
                resid, left[p], (((0,), (0,)), ((), ())), preferred_element_type=jnp.float32
            )
            grads.append((p, q, first, second))
        for p, q, first, second in grads:
            first_sum[p] += first
            second_sum[q] += second
        return carry

    lax.fori_loop(0, (live + GROUP - 1) // GROUP, step, 0)
    for index in range(4):
        near[index] = first_sum[2 * index]
        far[index] = first_sum[2 * index + 1].astype(jnp.bfloat16)
    d0[...] = second_sum[pl.ds(0, 8)]
    for index, out in enumerate((d1, d2, d3)):
        out[...] = second_sum[pl.ds(8 * (index + 1), 8)].astype(jnp.bfloat16)


def slot_grads(first_place, second_place, live, left_parts, right_parts, wins, losses):
    tile, width = left_parts[0].shape[1:]
    smem = pl.BlockSpec(memory_space=pltpu.SMEM)
    vmem = pl.BlockSpec(memory_space=pltpu.VMEM)

    def blocks(count, dtype):
        return jax.ShapeDtypeStruct((count, tile, width), dtype)

    return pl.pallas_call(
        slot_kernel,
        out_shape=(
            blocks(4, jnp.float32), blocks(4, jnp.bfloat16),
            blocks(8, jnp.float32), blocks(8, jnp.bfloat16), blocks(8, jnp.bfloat16), blocks(8, jnp.bfloat16),
        ),
        in_specs=[smem] * 3 + [vmem] * 10,
        out_specs=[vmem] * 6,
        scratch_shapes=[
            pltpu.VMEM((8, tile, width), jnp.bfloat16),
            pltpu.VMEM((8, tile, width), jnp.bfloat16),
            pltpu.VMEM((32, tile, width), jnp.bfloat16),
            pltpu.VMEM((8, tile, width), jnp.float32),
            pltpu.VMEM((32, tile, width), jnp.float32),
        ],
        compiler_params=pltpu.CompilerParams(vmem_limit_bytes=40 * 1024 * 1024),
    )(first_place, second_place, live, *left_parts, *right_parts, wins, losses)


def per_device(embedding, row_blocks, col_blocks, win_counts, loss_counts, live_tiles):
    at = {axis: lax.axis_index(axis) for axis in AXES}
    half = embedding.shape[1] // 2
    first_place = ((row_blocks // 2 - at["zl"]) % 4) * 2 + (row_blocks + at["core"]) % 2
    far_x = (col_blocks // 8 - at["x"]) % 4
    far_y = (col_blocks - at["y"]) % 4
    far_z = (col_blocks // 4 + at["zh"]) % 2
    outer = jnp.where(at["core"] == 0, far_y, far_x)
    inner = jnp.where(at["core"] == 0, far_x, far_y)
    second_place = (outer * 4 + inner) * 2 + far_z
    inner_axes, outer_axes = ("x", "y"), ("y", "x")

    current = embedding
    result = embedding.astype(jnp.float32)
    for iteration in range(ITERS):
        pair = jnp.stack([current, send(current, shift("zh", 1))])
        cores = jnp.stack([current, send(current, shift("core", 1))])
        inner_parts = [pair] + [send(pair, shift_by_core(inner_axes, -k)) for k in (1, 2, 3)]
        left_parts = [cores] + [send(cores, shift("zl", -k)) for k in (1, 2, 3)]
        line = jnp.concatenate(inner_parts)
        right_parts = [line] + [send(line, shift_by_core(outer_axes, -k)) for k in (1, 2, 3)]
        near, far, *second = slot_grads(
            first_place, second_place, live_tiles, left_parts, right_parts, win_counts, loss_counts
        )
        came = [send(second[k], shift_by_core(outer_axes, k)) for k in (1, 2, 3)]
        far = send(far, shift("core", 1))
        line_sum = second[0] + sum(part.astype(jnp.float32) for part in came)
        near = near + far.astype(jnp.float32)
        near_out = near.astype(jnp.bfloat16)
        line_out = line_sum.astype(jnp.bfloat16)
        came = [send(line_out[2 * k : 2 * k + 2], shift_by_core(inner_axes, k)) for k in (1, 2, 3)]
        near_came = [send(near_out[k], shift("zl", k)) for k in (1, 2, 3)]
        pair_sum = line_sum[:2] + sum(part.astype(jnp.float32) for part in came)
        partner = send(pair_sum[1].astype(jnp.bfloat16), shift("zh", 1))
        first_share = near[0] + sum(part.astype(jnp.float32) for part in near_came)
        raw = first_share - (pair_sum[0] + partner.astype(jnp.float32))
        grad = jnp.concatenate([raw[:, half:], -raw[:, :half]], axis=1)
        result = current.astype(jnp.float32) + RATE * grad
        current = result.astype(jnp.bfloat16)
    return result


def solution(mesh):
    fine = Mesh(mesh.devices.reshape(SIZES), AXES)
    rows = P(AXES)
    return jax.shard_map(
        per_device, mesh=fine, in_specs=(rows,) * 6, out_specs=rows, check_vma=False
    )
```

```python
import functools
import itertools

import jax
import jax.numpy as jnp
from jax import lax
from jax.experimental import pallas as pl
from jax.experimental.pallas import tpu as pltpu
from jax.sharding import Mesh
from jax.sharding import PartitionSpec as P

ITERS = 2
RATE = 0.01
GROUP = 4
AXES = ("zl", "core", "x", "zh", "y")
SIZES = (4, 2, 4, 2, 4)


def permutation(move):
    pairs = []
    for source, place in enumerate(itertools.product(*[range(size) for size in SIZES])):
        place = move(dict(zip(AXES, place)))
        target = 0
        for axis, size in zip(AXES, SIZES):
            target = target * size + place[axis] % size
        pairs.append((source, target))
    return pairs


def shift(axis, by):
    def move(place):
        place[axis] += by
        return place

    return permutation(move)


def shift_by_core(axes, by):
    def move(place):
        place[axes[place["core"]]] += by
        return place

    return permutation(move)


def send(values, pairs):
    return lax.ppermute(values, AXES, pairs)


def slot_kernel(
    first_ref, second_ref, live_ref,
    u0, u1, u2, u3, v0, v1, v2, v3, wins, losses,
    near, far, d0, d1, d2, d3,
    left, turned, right, first_sum, second_sum,
):
    half = left.shape[2] // 2
    for index, part in enumerate((u0, u1, u2, u3)):
        for core in range(2):
            block = part[core]
            left[2 * index + core] = block
            turned[2 * index + core, :, :half] = -block[:, half:]
            turned[2 * index + core, :, half:] = block[:, :half]
    for index, part in enumerate((v0, v1, v2, v3)):
        right[pl.ds(8 * index, 8)] = part[...]
    first_sum[...] = jnp.zeros_like(first_sum)
    second_sum[...] = jnp.zeros_like(second_sum)
    live = live_ref[0]

    def step(turn, carry):
        work = []
        for member in range(GROUP):
            slot = turn * GROUP + member
            p, q = first_ref[slot], second_ref[slot]
            score = lax.dot_general(
                turned[p], right[q], (((1,), (1,)), ((), ())), preferred_element_type=jnp.float32
            )
            won = wins[slot].astype(jnp.float32)
            lost = losses[slot].astype(jnp.float32)
            resid = won - (won + lost) * jax.nn.sigmoid(score)
            resid = jnp.where(slot < live, resid, 0.0).astype(jnp.bfloat16)
            work.append((p, q, resid))
        grads = []
        for p, q, resid in work:
            first = jnp.dot(resid, right[q], preferred_element_type=jnp.float32)
            second = lax.dot_general(
                resid, left[p], (((0,), (0,)), ((), ())), preferred_element_type=jnp.float32
            )
            grads.append((p, q, first, second))
        for p, q, first, second in grads:
            first_sum[p] += first
            second_sum[q] += second
        return carry

    lax.fori_loop(0, (live + GROUP - 1) // GROUP, step, 0)
    for index in range(4):
        near[index] = first_sum[2 * index]
        far[index] = first_sum[2 * index + 1].astype(jnp.bfloat16)
    d0[...] = second_sum[pl.ds(0, 8)]
    for index, out in enumerate((d1, d2, d3)):
        out[...] = second_sum[pl.ds(8 * (index + 1), 8)].astype(jnp.bfloat16)


def slot_grads(first_place, second_place, live, left_parts, right_parts, wins, losses):
    tile, width = left_parts[0].shape[1:]
    smem = pl.BlockSpec(memory_space=pltpu.SMEM)
    vmem = pl.BlockSpec(memory_space=pltpu.VMEM)

    def blocks(count, dtype):
        return jax.ShapeDtypeStruct((count, tile, width), dtype)

    return pl.pallas_call(
        slot_kernel,
        out_shape=(
            blocks(4, jnp.float32), blocks(4, jnp.bfloat16),
            blocks(8, jnp.float32), blocks(8, jnp.bfloat16), blocks(8, jnp.bfloat16), blocks(8, jnp.bfloat16),
        ),
        in_specs=[smem] * 3 + [vmem] * 10,
        out_specs=[vmem] * 6,
        scratch_shapes=[
            pltpu.VMEM((8, tile, width), jnp.bfloat16),
            pltpu.VMEM((8, tile, width), jnp.bfloat16),
            pltpu.VMEM((32, tile, width), jnp.bfloat16),
            pltpu.VMEM((8, tile, width), jnp.float32),
            pltpu.VMEM((32, tile, width), jnp.float32),
        ],
        compiler_params=pltpu.CompilerParams(vmem_limit_bytes=24 * 1024 * 1024),
    )(first_place, second_place, live, *left_parts, *right_parts, wins, losses)


def turn_back(raw):
    half = raw.shape[-1] // 2
    return jnp.concatenate([raw[..., half:], -raw[..., :half]], axis=-1)


def total(first, parts):
    return first + sum(part.astype(jnp.float32) for part in parts)


def per_device(embedding, row_blocks, col_blocks, win_counts, loss_counts, live_tiles):
    at = {axis: lax.axis_index(axis) for axis in AXES}
    first_place = ((row_blocks // 2 - at["zl"]) % 4) * 2 + (row_blocks + at["core"]) % 2
    far_x = (col_blocks // 8 - at["x"]) % 4
    far_y = (col_blocks - at["y"]) % 4
    far_z = (col_blocks // 4 + at["zh"]) % 2
    outer = jnp.where(at["core"] == 0, far_y, far_x)
    inner = jnp.where(at["core"] == 0, far_x, far_y)
    second_place = (outer * 4 + inner) * 2 + far_z
    inner_axes, outer_axes = ("x", "y"), ("y", "x")

    partner = send(embedding, shift("zh", 1))
    block, partner = lax.optimization_barrier((embedding, partner))
    pair = jnp.stack([block, partner])
    for iteration in range(ITERS):
        inner_parts = [pair] + [send(pair, shift_by_core(inner_axes, -k)) for k in (1, 2, 3)]
        cores = jnp.stack([block, send(block, shift("core", 1))])
        line = jnp.concatenate(inner_parts)
        line, cores = lax.optimization_barrier((line, cores))
        left_parts = [cores] + [send(cores, shift("zl", -k)) for k in (1, 2, 3)]
        right_parts = [line] + [send(line, shift_by_core(outer_axes, -k)) for k in (1, 2, 3)]
        near, far, *second = slot_grads(
            first_place, second_place, live_tiles, left_parts, right_parts, win_counts, loss_counts
        )
        came = [send(second[k], shift_by_core(outer_axes, k)) for k in (1, 2, 3)]
        near = near + send(far, shift("core", 1)).astype(jnp.float32)
        near_out = near.astype(jnp.bfloat16)
        first_share = total(near[0], [send(near_out[k], shift("zl", k)) for k in (1, 2, 3)])
        line_sum = total(second[0], came)
        line_out, first_share = lax.optimization_barrier((line_sum.astype(jnp.bfloat16), first_share))
        came = [send(line_out[2 * k : 2 * k + 2], shift_by_core(inner_axes, k)) for k in (1, 2, 3)]
        pair_sum = total(line_sum[:2], came)
        own, other = first_share - pair_sum[0], -pair_sum[1]
        if iteration == ITERS - 1:
            raw = own + send(other.astype(jnp.bfloat16), shift("zh", 1)).astype(jnp.float32)
            return block.astype(jnp.float32) + RATE * turn_back(raw)
        pieces = lax.optimization_barrier(jnp.stack([own, other]).astype(jnp.bfloat16))
        swapped = send(pieces, shift("zh", 1))
        raw = pieces.astype(jnp.float32) + swapped[::-1].astype(jnp.float32)
        pair = (pair.astype(jnp.float32) + RATE * turn_back(raw)).astype(jnp.bfloat16)
        block = pair[0]


def solution(mesh):
    fine = Mesh(mesh.devices.reshape(SIZES), AXES)
    rows = P(AXES)
    return jax.shard_map(
        per_device, mesh=fine, in_specs=(rows,) * 6, out_specs=rows, check_vma=False
    )
```

```python
import functools
import itertools

import jax
import jax.numpy as jnp
from jax import lax
from jax.experimental import pallas as pl
from jax.experimental.pallas import tpu as pltpu
from jax.sharding import Mesh
from jax.sharding import PartitionSpec as P

ITERS = 2
RATE = 0.01
GROUP = 4
AXES = ("zl", "core", "x", "zh", "y")
SIZES = (4, 2, 4, 2, 4)


def permutation(move):
    pairs = []
    for source, place in enumerate(itertools.product(*[range(size) for size in SIZES])):
        place = move(dict(zip(AXES, place)))
        target = 0
        for axis, size in zip(AXES, SIZES):
            target = target * size + place[axis] % size
        pairs.append((source, target))
    return pairs


def shift(axis, by):
    def move(place):
        place[axis] += by
        return place

    return permutation(move)


def shift_by_core(axes, by):
    def move(place):
        place[axes[place["core"]]] += by
        return place

    return permutation(move)


def send(values, pairs):
    return lax.ppermute(values, AXES, pairs)


def list_slots(second_ref, live, slots, begin, end, slot_count):
    count = jnp.int32(0)
    for slot in range(slot_count):
        slots[count] = slot
        here = (second_ref[slot] >= begin) & (second_ref[slot] < end) & (slot < live)
        count = count + here.astype(jnp.int32)
    for extra in range(GROUP):
        slots[count + extra] = 0
    return count


def visit_slots(
    first_ref, second_ref, live_ref, slots, begin, end, left, turned, right, wins, losses, first_sum, second_sum
):
    count = list_slots(second_ref, live_ref[0], slots, begin, end, wins.shape[0])

    def step(turn, carry):
        work = []
        for member in range(GROUP):
            place = turn * GROUP + member
            slot = slots[place]
            p = first_ref[slot]
            q = jnp.clip(second_ref[slot] - begin, 0, end - begin - 1)
            score = lax.dot_general(
                turned[p], right[q], (((1,), (1,)), ((), ())), preferred_element_type=jnp.float32
            )
            won = wins[slot].astype(jnp.float32)
            lost = losses[slot].astype(jnp.float32)
            resid = won - (won + lost) * jax.nn.sigmoid(score)
            resid = jnp.where(place < count, resid, 0.0).astype(jnp.bfloat16)
            work.append((p, q, resid))
        grads = []
        for p, q, resid in work:
            first = jnp.dot(resid, right[q], preferred_element_type=jnp.float32)
            second = lax.dot_general(
                resid, left[p], (((0,), (0,)), ((), ())), preferred_element_type=jnp.float32
            )
            grads.append((p, q, first, second))
        for p, q, first, second in grads:
            first_sum[p] += first
            second_sum[q] += second
        return carry

    lax.fori_loop(0, (count + GROUP - 1) // GROUP, step, 0)


def own_kernel(
    first_ref, second_ref, live_ref, u0, u1, u2, u3, right, wins, losses,
    left, turned, first_sum, second_sum, slots,
):
    half = left.shape[2] // 2
    for place, part in zip((0, 1, 4, 5), (u0, u1, u2, u3)):
        here = pl.ds(place, part.shape[0])
        left[here] = part[...]
        turned[here, :, :half] = -part[:, :, half:]
        turned[here, :, half:] = part[:, :, :half]
    first_sum[...] = jnp.zeros_like(first_sum)
    second_sum[...] = jnp.zeros_like(second_sum)
    visit_slots(
        first_ref, second_ref, live_ref, slots, 0, 8, left, turned, right, wins, losses, first_sum, second_sum
    )


def rest_kernel(
    first_ref, second_ref, live_ref, left, turned, first_in, v1, v2, v3, wins, losses,
    near, far, d1, d2, d3, slots, right, first_sum, second_sum,
):
    for index, part in enumerate((v1, v2, v3)):
        right[pl.ds(8 * index, 8)] = part[...]
    first_sum[...] = first_in[...]
    second_sum[...] = jnp.zeros_like(second_sum)
    visit_slots(
        first_ref, second_ref, live_ref, slots, 8, 32, left, turned, right, wins, losses, first_sum, second_sum
    )
    for index, out in enumerate((d1, d2, d3)):
        out[...] = second_sum[pl.ds(8 * index, 8)].astype(jnp.bfloat16)
    near[...] = first_sum[:4]
    far[...] = first_sum[4:].astype(jnp.bfloat16)


def call(kernel, places, operands, outs, scratch, tile, width):
    smem = pl.BlockSpec(memory_space=pltpu.SMEM)
    vmem = pl.BlockSpec(memory_space=pltpu.VMEM)
    slot_count = operands[-1].shape[0]
    return pl.pallas_call(
        kernel,
        out_shape=[jax.ShapeDtypeStruct((count, tile, width), dtype) for count, dtype in outs],
        in_specs=[smem] * 3 + [vmem] * len(operands),
        out_specs=[vmem] * len(outs),
        scratch_shapes=[pltpu.SMEM((slot_count + GROUP,), jnp.int32)]
        + [pltpu.VMEM((count, tile, width), dtype) for count, dtype in scratch],
        compiler_params=pltpu.CompilerParams(vmem_limit_bytes=16 * 1024 * 1024),
    )(*places, *operands)


def turn_back(raw):
    half = raw.shape[-1] // 2
    return jnp.concatenate([raw[..., half:], -raw[..., :half]], axis=-1)


def total(first, parts):
    return first + sum(part.astype(jnp.float32) for part in parts)


def per_device(embedding, row_blocks, col_blocks, win_counts, loss_counts, live_tiles):
    at = {axis: lax.axis_index(axis) for axis in AXES}
    first_place = (row_blocks // 2 - at["zl"]) % 4 + (row_blocks + at["core"]) % 2 * 4
    far_x = (col_blocks // 8 - at["x"]) % 4
    far_y = (col_blocks - at["y"]) % 4
    far_z = (col_blocks // 4 + at["zh"]) % 2
    outer = jnp.where(at["core"] == 0, far_y, far_x)
    inner = jnp.where(at["core"] == 0, far_x, far_y)
    second_place = (outer * 4 + inner) * 2 + far_z
    inner_axes, outer_axes = ("x", "y"), ("y", "x")

    block = embedding
    partner = send(block, shift("zh", 1))
    pair = jnp.stack([block, partner])
    block, partner = lax.optimization_barrier((block, partner))
    for iteration in range(ITERS):
        inner_parts = {k: send(pair, shift_by_core(inner_axes, -k)) for k in (1, 3, 2)}
        inner_parts = [pair] + [inner_parts[k] for k in (1, 2, 3)]
        other = send(block, shift("core", 1))
        line = jnp.concatenate(inner_parts)
        line, block, other = lax.optimization_barrier((line, block, other))
        mine = jnp.stack([send(block, shift("zl", -k)) for k in (1, 2, 3)])
        theirs = send(mine, shift("core", 1))
        left_parts = (block[None], mine, other[None], theirs)
        right_parts = {k: send(line, shift_by_core(outer_axes, -k)) for k in (1, 3, 2)}
        right_parts = [line] + [right_parts[k] for k in (1, 2, 3)]
        places = (first_place, second_place, live_tiles)
        tile, width = block.shape
        left, turned, first_sum, line_sum = call(
            own_kernel,
            places,
            (*left_parts, right_parts[0], win_counts, loss_counts),
            [(8, jnp.bfloat16), (8, jnp.bfloat16), (8, jnp.float32), (8, jnp.float32)],
            [],
            tile,
            width,
        )
        near, far, *second = call(
            rest_kernel,
            places,
            (left, turned, first_sum, *right_parts[1:], win_counts, loss_counts),
            [(4, jnp.float32), (4, jnp.bfloat16)] + [(8, jnp.bfloat16)] * 3,
            [(24, jnp.bfloat16), (8, jnp.float32), (24, jnp.float32)],
            tile,
            width,
        )
        second = [line_sum] + second
        came = [send(second[k], shift_by_core(outer_axes, k)) for k in (2, 1, 3)]
        near = near + send(far, shift("core", 1)).astype(jnp.float32)
        near_out = near.astype(jnp.bfloat16)
        first_share = total(near[0], [send(near_out[k], shift("zl", k)) for k in (1, 2, 3)])
        line_sum = total(second[0], came)
        line_out, first_share = lax.optimization_barrier((line_sum.astype(jnp.bfloat16), first_share))
        came = [send(line_out[2 * k : 2 * k + 2], shift_by_core(inner_axes, k)) for k in (2, 1, 3)]
        pair_sum = total(line_sum[:2], came)
        own, other = first_share - pair_sum[0], -pair_sum[1]
        if iteration == ITERS - 1:
            raw = own + send(other.astype(jnp.bfloat16), shift("zh", 1)).astype(jnp.float32)
            return block.astype(jnp.float32) + RATE * turn_back(raw)
        pieces = lax.optimization_barrier(jnp.stack([other, own]).astype(jnp.bfloat16))
        raw = jnp.stack([own, other]) + send(pieces, shift("zh", 1)).astype(jnp.float32)
        pair = (pair.astype(jnp.float32) + RATE * turn_back(raw)).astype(jnp.bfloat16)
        block = pair[0]


def solution(mesh):
    fine = Mesh(mesh.devices.reshape(SIZES), AXES)
    rows = P(AXES)
    return jax.shard_map(
        per_device, mesh=fine, in_specs=(rows,) * 6, out_specs=rows, check_vma=False
    )
```

```python
import functools
import itertools

import jax
import jax.numpy as jnp
from jax import lax
from jax.experimental import pallas as pl
from jax.experimental.pallas import tpu as pltpu
from jax.sharding import Mesh
from jax.sharding import PartitionSpec as P

ITERS = 2
RATE = 0.01
GROUP = 8
AXES = ("zl", "core", "x", "zh", "y")
SIZES = (4, 2, 4, 2, 4)


def permutation(move):
    pairs = []
    for source, place in enumerate(itertools.product(*[range(size) for size in SIZES])):
        place = move(dict(zip(AXES, place)))
        target = 0
        for axis, size in zip(AXES, SIZES):
            target = target * size + place[axis] % size
        pairs.append((source, target))
    return pairs


def shift(axis, by):
    def move(place):
        place[axis] += by
        return place

    return permutation(move)


def shift_by_core(axes, by):
    def move(place):
        place[axes[place["core"]]] += by
        return place

    return permutation(move)


def send(values, pairs):
    return lax.ppermute(values, AXES, pairs)


def list_slots(second_ref, live, slots, begin, end, slot_count):
    count = jnp.int32(0)
    for slot in range(slot_count):
        slots[count] = slot
        here = (second_ref[slot] >= begin) & (second_ref[slot] < end) & (slot < live)
        count = count + here.astype(jnp.int32)
    for extra in range(GROUP):
        slots[count + extra] = 0
    return count


def visit_slots(
    first_ref, second_ref, live_ref, slots, begin, end, left, turned, right, wins, losses, first_sum, second_sum
):
    count = list_slots(second_ref, live_ref[0], slots, begin, end, wins.shape[0])

    def step(turn, carry):
        work = []
        for member in range(GROUP):
            place = turn * GROUP + member
            slot = slots[place]
            p = first_ref[slot]
            q = jnp.clip(second_ref[slot] - begin, 0, end - begin - 1)
            score = lax.dot_general(
                turned[p], right[q], (((1,), (1,)), ((), ())), preferred_element_type=jnp.float32
            )
            won = wins[slot].astype(jnp.float32)
            lost = losses[slot].astype(jnp.float32)
            resid = won - (won + lost) * jax.nn.sigmoid(score)
            resid = jnp.where(place < count, resid, 0.0).astype(jnp.bfloat16)
            work.append((p, q, resid))
        grads = []
        for p, q, resid in work:
            first = jnp.dot(resid, right[q], preferred_element_type=jnp.float32)
            second = lax.dot_general(
                resid, left[p], (((0,), (0,)), ((), ())), preferred_element_type=jnp.float32
            )
            grads.append((p, q, first, second))
        for p, q, first, second in grads:
            first_sum[p] += first
            second_sum[q] += second
        return carry

    lax.fori_loop(0, (count + GROUP - 1) // GROUP, step, 0)


def own_kernel(
    first_ref, second_ref, live_ref, u0, u1, u2, u3, right, wins, losses,
    left, turned, first_sum, second_sum, slots,
):
    half = left.shape[2] // 2
    for place, part in zip((0, 1, 4, 5), (u0, u1, u2, u3)):
        here = pl.ds(place, part.shape[0])
        left[here] = part[...]
        turned[here, :, :half] = -part[:, :, half:]
        turned[here, :, half:] = part[:, :, :half]
    first_sum[...] = jnp.zeros_like(first_sum)
    second_sum[...] = jnp.zeros_like(second_sum)
    visit_slots(
        first_ref, second_ref, live_ref, slots, 0, 8, left, turned, right, wins, losses, first_sum, second_sum
    )


def rest_kernel(
    first_ref, second_ref, live_ref, left, turned, first_in, v1, v2, v3, wins, losses,
    near, far, d1, d2, d3, slots, right, first_sum, second_sum,
):
    for index, part in enumerate((v1, v2, v3)):
        right[pl.ds(8 * index, 8)] = part[...]
    first_sum[...] = first_in[...]
    second_sum[...] = jnp.zeros_like(second_sum)
    visit_slots(
        first_ref, second_ref, live_ref, slots, 8, 32, left, turned, right, wins, losses, first_sum, second_sum
    )
    for index, out in enumerate((d1, d2, d3)):
        out[...] = second_sum[pl.ds(8 * index, 8)].astype(jnp.bfloat16)
    near[...] = first_sum[:4]
    far[...] = first_sum[4:].astype(jnp.bfloat16)


def call(kernel, places, operands, outs, scratch, tile, width):
    smem = pl.BlockSpec(memory_space=pltpu.SMEM)
    vmem = pl.BlockSpec(memory_space=pltpu.VMEM)
    slot_count = operands[-1].shape[0]
    return pl.pallas_call(
        kernel,
        out_shape=[jax.ShapeDtypeStruct((count, tile, width), dtype) for count, dtype in outs],
        in_specs=[smem] * 3 + [vmem] * len(operands),
        out_specs=[vmem] * len(outs),
        scratch_shapes=[pltpu.SMEM((slot_count + GROUP,), jnp.int32)]
        + [pltpu.VMEM((count, tile, width), dtype) for count, dtype in scratch],
        compiler_params=pltpu.CompilerParams(vmem_limit_bytes=16 * 1024 * 1024),
    )(*places, *operands)


def turn_back(raw):
    half = raw.shape[-1] // 2
    return jnp.concatenate([raw[..., half:], -raw[..., :half]], axis=-1)


def total(first, parts):
    return first + sum(part.astype(jnp.float32) for part in parts)


def per_device(embedding, row_blocks, col_blocks, win_counts, loss_counts, live_tiles):
    at = {axis: lax.axis_index(axis) for axis in AXES}
    first_place = (row_blocks // 2 - at["zl"]) % 4 + (row_blocks + at["core"]) % 2 * 4
    far_x = (col_blocks // 8 - at["x"]) % 4
    far_y = (col_blocks - at["y"]) % 4
    far_z = (col_blocks // 4 + at["zh"]) % 2
    outer = jnp.where(at["core"] == 0, far_y, far_x)
    inner = jnp.where(at["core"] == 0, far_x, far_y)
    second_place = (outer * 4 + inner) * 2 + far_z
    inner_axes, outer_axes = ("x", "y"), ("y", "x")

    block = embedding
    partner = send(block, shift("zh", 1))
    pair = jnp.stack([block, partner])
    block, partner, first_place, second_place = lax.optimization_barrier(
        (block, partner, first_place, second_place)
    )
    for iteration in range(ITERS):
        inner_parts = {k: send(pair, shift_by_core(inner_axes, -k)) for k in (1, 3, 2)}
        inner_parts = [pair] + [inner_parts[k] for k in (1, 2, 3)]
        other = send(block, shift("core", 1))
        line = jnp.concatenate(inner_parts)
        line, block, other = lax.optimization_barrier((line, block, other))
        mine = jnp.stack([send(block, shift("zl", -k)) for k in (1, 2, 3)])
        theirs = send(mine, shift("core", 1))
        left_parts = (block[None], mine, other[None], theirs)
        right_parts = {k: send(line, shift_by_core(outer_axes, -k)) for k in (1, 3, 2)}
        right_parts = [line] + [right_parts[k] for k in (1, 2, 3)]
        places = (first_place, second_place, live_tiles)
        tile, width = block.shape
        left, turned, first_sum, line_sum = call(
            own_kernel,
            places,
            (*left_parts, right_parts[0], win_counts, loss_counts),
            [(8, jnp.bfloat16), (8, jnp.bfloat16), (8, jnp.float32), (8, jnp.float32)],
            [],
            tile,
            width,
        )
        near, far, *second = call(
            rest_kernel,
            places,
            (left, turned, first_sum, *right_parts[1:], win_counts, loss_counts),
            [(4, jnp.float32), (4, jnp.bfloat16)] + [(8, jnp.bfloat16)] * 3,
            [(24, jnp.bfloat16), (8, jnp.float32), (24, jnp.float32)],
            tile,
            width,
        )
        second = [line_sum] + second
        came = [send(second[k], shift_by_core(outer_axes, k)) for k in (2, 1, 3)]
        near = near + send(far, shift("core", 1)).astype(jnp.float32)
        near_out = near.astype(jnp.bfloat16)
        first_share = total(near[0], [send(near_out[k], shift("zl", k)) for k in (1, 2, 3)])
        line_sum = total(second[0], came)
        line_out, first_share = lax.optimization_barrier((line_sum.astype(jnp.bfloat16), first_share))
        came = [send(line_out[2 * k : 2 * k + 2], shift_by_core(inner_axes, k)) for k in (2, 1, 3)]
        pair_sum = total(line_sum[:2], came)
        own, other = first_share - pair_sum[0], -pair_sum[1]
        if iteration == ITERS - 1:
            raw = own + send(other.astype(jnp.bfloat16), shift("zh", 1)).astype(jnp.float32)
            return block.astype(jnp.float32) + RATE * turn_back(raw)
        pieces = lax.optimization_barrier(jnp.stack([other, own]).astype(jnp.bfloat16))
        raw = jnp.stack([own, other]) + send(pieces, shift("zh", 1)).astype(jnp.float32)
        pair = (pair.astype(jnp.float32) + RATE * turn_back(raw)).astype(jnp.bfloat16)
        block = pair[0]


def solution(mesh):
    fine = Mesh(mesh.devices.reshape(SIZES), AXES)
    rows = P(AXES)
    return jax.shard_map(
        per_device, mesh=fine, in_specs=(rows,) * 6, out_specs=rows, check_vma=False
    )
```

```python
import functools
import itertools

import jax
import jax.numpy as jnp
from jax import lax
from jax.experimental import pallas as pl
from jax.experimental.pallas import tpu as pltpu
from jax.sharding import Mesh
from jax.sharding import PartitionSpec as P

ITERS = 2
RATE = 0.01
OWN_GROUP, GROUP = 4, 8
AXES = ("zl", "core", "x", "zh", "y")
SIZES = (4, 2, 4, 2, 4)


def permutation(move):
    pairs = []
    for source, place in enumerate(itertools.product(*[range(size) for size in SIZES])):
        place = move(dict(zip(AXES, place)))
        target = 0
        for axis, size in zip(AXES, SIZES):
            target = target * size + place[axis] % size
        pairs.append((source, target))
    return pairs


def shift(axis, by):
    def move(place):
        place[axis] += by
        return place

    return permutation(move)


def shift_by_core(axes, by):
    def move(place):
        place[axes[place["core"]]] += by
        return place

    return permutation(move)


def send(values, pairs):
    return lax.ppermute(values, AXES, pairs)


def list_slots(second_ref, live, slots, begin, end, slot_count):
    count = jnp.int32(0)
    for slot in range(slot_count):
        slots[count] = slot
        here = (second_ref[slot] >= begin) & (second_ref[slot] < end) & (slot < live)
        count = count + here.astype(jnp.int32)
    for extra in range(GROUP):
        slots[count + extra] = 0
    return count


def visit_slots(
    first_ref, second_ref, live_ref, slots, begin, end, left, turned, right, wins, losses, first_sum, second_sum,
    group=GROUP,
):
    count = list_slots(second_ref, live_ref[0], slots, begin, end, wins.shape[0])

    def step(turn, carry):
        work = []
        for member in range(group):
            place = turn * group + member
            slot = slots[place]
            p = first_ref[slot]
            q = jnp.clip(second_ref[slot] - begin, 0, end - begin - 1)
            score = lax.dot_general(
                turned[p], right[q], (((1,), (1,)), ((), ())), preferred_element_type=jnp.float32
            )
            won = wins[slot].astype(jnp.float32)
            lost = losses[slot].astype(jnp.float32)
            resid = won - (won + lost) * jax.nn.sigmoid(score)
            resid = jnp.where(place < count, resid, 0.0).astype(jnp.bfloat16)
            work.append((p, q, resid))
        grads = []
        for p, q, resid in work:
            first = jnp.dot(resid, right[q], preferred_element_type=jnp.float32)
            second = lax.dot_general(
                resid, left[p], (((0,), (0,)), ((), ())), preferred_element_type=jnp.float32
            )
            grads.append((p, q, first, second))
        for p, q, first, second in grads:
            first_sum[p] += first
            second_sum[q] += second
        return carry

    lax.fori_loop(0, (count + group - 1) // group, step, 0)


def own_kernel(
    first_ref, second_ref, live_ref, u0, u1, u2, u3, right, wins, losses,
    left, turned, first_sum, second_sum, slots,
):
    half = left.shape[2] // 2
    for place, part in zip((0, 1, 4, 5), (u0, u1, u2, u3)):
        here = pl.ds(place, part.shape[0])
        left[here] = part[...]
        turned[here, :, :half] = -part[:, :, half:]
        turned[here, :, half:] = part[:, :, :half]
    first_sum[...] = jnp.zeros_like(first_sum)
    second_sum[...] = jnp.zeros_like(second_sum)
    visit_slots(
        first_ref, second_ref, live_ref, slots, 0, 8, left, turned, right, wins, losses, first_sum, second_sum,
        group=OWN_GROUP,
    )


def rest_kernel(
    first_ref, second_ref, live_ref, left, turned, first_in, v1, v2, v3, wins, losses,
    near, far, d1, d2, d3, slots, right, first_sum, second_sum,
):
    for index, part in enumerate((v1, v2, v3)):
        right[pl.ds(8 * index, 8)] = part[...]
    first_sum[...] = first_in[...]
    second_sum[...] = jnp.zeros_like(second_sum)
    visit_slots(
        first_ref, second_ref, live_ref, slots, 8, 32, left, turned, right, wins, losses, first_sum, second_sum
    )
    for index, out in enumerate((d1, d2, d3)):
        out[...] = second_sum[pl.ds(8 * index, 8)].astype(jnp.bfloat16)
    near[...] = first_sum[:4]
    far[...] = first_sum[4:].astype(jnp.bfloat16)


def call(kernel, places, operands, outs, scratch, tile, width):
    smem = pl.BlockSpec(memory_space=pltpu.SMEM)
    vmem = pl.BlockSpec(memory_space=pltpu.VMEM)
    slot_count = operands[-1].shape[0]
    return pl.pallas_call(
        kernel,
        out_shape=[jax.ShapeDtypeStruct((count, tile, width), dtype) for count, dtype in outs],
        in_specs=[smem] * 3 + [vmem] * len(operands),
        out_specs=[vmem] * len(outs),
        scratch_shapes=[pltpu.SMEM((slot_count + GROUP,), jnp.int32)]
        + [pltpu.VMEM((count, tile, width), dtype) for count, dtype in scratch],
        compiler_params=pltpu.CompilerParams(vmem_limit_bytes=16 * 1024 * 1024),
    )(*places, *operands)


def turn_back(raw):
    half = raw.shape[-1] // 2
    return jnp.concatenate([raw[..., half:], -raw[..., :half]], axis=-1)


def total(first, parts):
    return first + sum(part.astype(jnp.float32) for part in parts)


def per_device(embedding, row_blocks, col_blocks, win_counts, loss_counts, live_tiles):
    at = {axis: lax.axis_index(axis) for axis in AXES}
    first_place = (row_blocks // 2 - at["zl"]) % 4 + (row_blocks + at["core"]) % 2 * 4
    far_x = (col_blocks // 8 - at["x"]) % 4
    far_y = (col_blocks - at["y"]) % 4
    far_z = (col_blocks // 4 + at["zh"]) % 2
    outer = jnp.where(at["core"] == 0, far_y, far_x)
    inner = jnp.where(at["core"] == 0, far_x, far_y)
    second_place = (outer * 4 + inner) * 2 + far_z
    inner_axes, outer_axes = ("x", "y"), ("y", "x")

    block = embedding
    partner = send(block, shift("zh", 1))
    pair = jnp.stack([block, partner])
    block, partner, first_place, second_place = lax.optimization_barrier(
        (block, partner, first_place, second_place)
    )
    for iteration in range(ITERS):
        inner_parts = {k: send(pair, shift_by_core(inner_axes, -k)) for k in (1, 3, 2)}
        inner_parts = [pair] + [inner_parts[k] for k in (1, 2, 3)]
        other = send(block, shift("core", 1))
        line = jnp.concatenate(inner_parts)
        line, block, other = lax.optimization_barrier((line, block, other))
        mine = jnp.stack([send(block, shift("zl", -k)) for k in (1, 2, 3)])
        theirs = send(mine, shift("core", 1))
        left_parts = (block[None], mine, other[None], theirs)
        right_parts = {k: send(line, shift_by_core(outer_axes, -k)) for k in (1, 3, 2)}
        right_parts = [line] + [right_parts[k] for k in (1, 2, 3)]
        places = (first_place, second_place, live_tiles)
        tile, width = block.shape
        left, turned, first_sum, line_sum = call(
            own_kernel,
            places,
            (*left_parts, right_parts[0], win_counts, loss_counts),
            [(8, jnp.bfloat16), (8, jnp.bfloat16), (8, jnp.float32), (8, jnp.float32)],
            [],
            tile,
            width,
        )
        near, far, *second = call(
            rest_kernel,
            places,
            (left, turned, first_sum, *right_parts[1:], win_counts, loss_counts),
            [(4, jnp.float32), (4, jnp.bfloat16)] + [(8, jnp.bfloat16)] * 3,
            [(24, jnp.bfloat16), (8, jnp.float32), (24, jnp.float32)],
            tile,
            width,
        )
        second = [line_sum] + second
        came = [send(second[k], shift_by_core(outer_axes, k)) for k in (2, 1, 3)]
        near = near + send(far, shift("core", 1)).astype(jnp.float32)
        near_out = near.astype(jnp.bfloat16)
        first_share = total(near[0], [send(near_out[k], shift("zl", k)) for k in (1, 2, 3)])
        line_sum = total(second[0], came)
        line_out, first_share = lax.optimization_barrier((line_sum.astype(jnp.bfloat16), first_share))
        came = [send(line_out[2 * k : 2 * k + 2], shift_by_core(inner_axes, k)) for k in (2, 1, 3)]
        pair_sum = total(line_sum[:2], came)
        own, other = first_share - pair_sum[0], -pair_sum[1]
        if iteration == ITERS - 1:
            raw = own + send(other.astype(jnp.bfloat16), shift("zh", 1)).astype(jnp.float32)
            return block.astype(jnp.float32) + RATE * turn_back(raw)
        pieces = lax.optimization_barrier(jnp.stack([other, own]).astype(jnp.bfloat16))
        raw = jnp.stack([own, other]) + send(pieces, shift("zh", 1)).astype(jnp.float32)
        pair = (pair.astype(jnp.float32) + RATE * turn_back(raw)).astype(jnp.bfloat16)
        block = pair[0]


def solution(mesh):
    fine = Mesh(mesh.devices.reshape(SIZES), AXES)
    rows = P(AXES)
    return jax.shard_map(
        per_device, mesh=fine, in_specs=(rows,) * 6, out_specs=rows, check_vma=False
    )
```

```python
import functools
import itertools

import jax
import jax.numpy as jnp
from jax import lax
from jax.experimental import pallas as pl
from jax.experimental.pallas import tpu as pltpu
from jax.sharding import Mesh
from jax.sharding import PartitionSpec as P

ITERS = 2
RATE = 0.01
GROUP = 8
AXES = ("zl", "core", "x", "zh", "y")
SIZES = (4, 2, 4, 2, 4)


def permutation(move):
    pairs = []
    for source, place in enumerate(itertools.product(*[range(size) for size in SIZES])):
        place = move(dict(zip(AXES, place)))
        target = 0
        for axis, size in zip(AXES, SIZES):
            target = target * size + place[axis] % size
        pairs.append((source, target))
    return pairs


def shift(axis, by):
    def move(place):
        place[axis] += by
        return place

    return permutation(move)


def shift_by_core(axes, by):
    def move(place):
        place[axes[place["core"]]] += by
        return place

    return permutation(move)


def send(values, pairs):
    return lax.ppermute(values, AXES, pairs)


def list_slots(second_ref, live, slots, begin, end, slot_count):
    count = jnp.int32(0)
    for slot in range(slot_count):
        slots[count] = slot
        here = (second_ref[slot] >= begin) & (second_ref[slot] < end) & (slot < live)
        count = count + here.astype(jnp.int32)
    for extra in range(GROUP):
        slots[count + extra] = 0
    return count


def visit_slots(
    first_ref, second_ref, live_ref, slots, begin, end, left, turned, right, wins, losses, first_sum, second_sum
):
    count = list_slots(second_ref, live_ref[0], slots, begin, end, wins.shape[0])

    def step(turn, carry):
        work = []
        for member in range(GROUP):
            place = turn * GROUP + member
            slot = slots[place]
            p = first_ref[slot]
            q = jnp.clip(second_ref[slot] - begin, 0, end - begin - 1)
            score = lax.dot_general(
                turned[p], right[q], (((1,), (1,)), ((), ())), preferred_element_type=jnp.float32
            )
            won = wins[slot].astype(jnp.float32)
            lost = losses[slot].astype(jnp.float32)
            resid = won - (won + lost) * jax.nn.sigmoid(score)
            resid = jnp.where(place < count, resid, 0.0).astype(jnp.bfloat16)
            work.append((p, q, resid))
        grads = []
        for p, q, resid in work:
            first = jnp.dot(resid, right[q], preferred_element_type=jnp.float32)
            second = lax.dot_general(
                resid, left[p], (((0,), (0,)), ((), ())), preferred_element_type=jnp.float32
            )
            grads.append((p, q, first, second))
        for p, q, first, second in grads:
            first_sum[p] += first
            second_sum[q] += second
        return carry

    lax.fori_loop(0, (count + GROUP - 1) // GROUP, step, 0)


def own_kernel(
    first_ref, second_ref, live_ref, u0, u1, u2, u3, right, wins, losses,
    left, turned, first_sum, second_sum, slots,
):
    half = left.shape[2] // 2
    for place, part in zip((0, 1, 4, 5), (u0, u1, u2, u3)):
        here = pl.ds(place, part.shape[0])
        left[here] = part[...]
        turned[here, :, :half] = -part[:, :, half:]
        turned[here, :, half:] = part[:, :, :half]
    first_sum[...] = jnp.zeros_like(first_sum)
    second_sum[...] = jnp.zeros_like(second_sum)
    visit_slots(
        first_ref, second_ref, live_ref, slots, 0, 8, left, turned, right, wins, losses, first_sum, second_sum
    )


def rest_kernel(
    first_ref, second_ref, live_ref, left, turned, first_in, v1, v2, v3, wins, losses,
    near, far, d1, d2, d3, slots, right, first_sum, second_sum,
):
    for index, part in enumerate((v1, v2, v3)):
        right[pl.ds(8 * index, 8)] = part[...]
    first_sum[...] = first_in[...]
    second_sum[...] = jnp.zeros_like(second_sum)
    visit_slots(
        first_ref, second_ref, live_ref, slots, 8, 32, left, turned, right, wins, losses, first_sum, second_sum
    )
    for index, out in enumerate((d1, d2, d3)):
        out[...] = second_sum[pl.ds(8 * index, 8)].astype(jnp.bfloat16)
    near[...] = first_sum[:4]
    far[...] = first_sum[4:].astype(jnp.bfloat16)


def call(kernel, places, operands, outs, scratch, tile, width):
    smem = pl.BlockSpec(memory_space=pltpu.SMEM)
    vmem = pl.BlockSpec(memory_space=pltpu.VMEM)
    slot_count = operands[-1].shape[0]
    return pl.pallas_call(
        kernel,
        out_shape=[jax.ShapeDtypeStruct((count, tile, width), dtype) for count, dtype in outs],
        in_specs=[smem] * 3 + [vmem] * len(operands),
        out_specs=[vmem] * len(outs),
        scratch_shapes=[pltpu.SMEM((slot_count + GROUP,), jnp.int32)]
        + [pltpu.VMEM((count, tile, width), dtype) for count, dtype in scratch],
        compiler_params=pltpu.CompilerParams(vmem_limit_bytes=16 * 1024 * 1024),
    )(*places, *operands)


def turn_back(raw):
    half = raw.shape[-1] // 2
    return jnp.concatenate([raw[..., half:], -raw[..., :half]], axis=-1)


def total(first, parts):
    return first + sum(part.astype(jnp.float32) for part in parts)


def per_device(embedding, row_blocks, col_blocks, win_counts, loss_counts, live_tiles):
    at = {axis: lax.axis_index(axis) for axis in AXES}
    first_place = (row_blocks // 2 - at["zl"]) % 4 + (row_blocks + at["core"]) % 2 * 4
    far_x = (col_blocks // 8 - at["x"]) % 4
    far_y = (col_blocks - at["y"]) % 4
    far_z = (col_blocks // 4 + at["zh"]) % 2
    outer = jnp.where(at["core"] == 0, far_y, far_x)
    inner = jnp.where(at["core"] == 0, far_x, far_y)
    second_place = (outer * 4 + inner) * 2 + far_z
    inner_axes, outer_axes = ("x", "y"), ("y", "x")

    block = embedding
    partner = send(block, shift("zh", 1))
    pair = jnp.stack([block, partner])
    block, partner, first_place, second_place = lax.optimization_barrier(
        (block, partner, first_place, second_place)
    )
    for iteration in range(ITERS):
        inner_parts = {k: send(pair, shift_by_core(inner_axes, -k)) for k in (1, 3, 2)}
        inner_parts = [pair] + [inner_parts[k] for k in (1, 2, 3)]
        other = send(block, shift("core", 1))
        line = jnp.concatenate(inner_parts)
        line, block, other = lax.optimization_barrier((line, block, other))
        mine = {k: send(block, shift("zl", -k)) for k in (2, 1, 3)}
        mine = jnp.stack([mine[k] for k in (1, 2, 3)])
        theirs = send(mine, shift("core", 1))
        left_parts = (block[None], mine, other[None], theirs)
        right_parts = {k: send(line, shift_by_core(outer_axes, -k)) for k in (1, 3, 2)}
        right_parts = [line] + [right_parts[k] for k in (1, 2, 3)]
        places = (first_place, second_place, live_tiles)
        tile, width = block.shape
        left, turned, first_sum, line_sum = call(
            own_kernel,
            places,
            (*left_parts, right_parts[0], win_counts, loss_counts),
            [(8, jnp.bfloat16), (8, jnp.bfloat16), (8, jnp.float32), (8, jnp.float32)],
            [],
            tile,
            width,
        )
        near, far, *second = call(
            rest_kernel,
            places,
            (left, turned, first_sum, *right_parts[1:], win_counts, loss_counts),
            [(4, jnp.float32), (4, jnp.bfloat16)] + [(8, jnp.bfloat16)] * 3,
            [(24, jnp.bfloat16), (8, jnp.float32), (24, jnp.float32)],
            tile,
            width,
        )
        second = [line_sum] + second
        came = [send(second[k], shift_by_core(outer_axes, k)) for k in (2, 1, 3)]
        near = near + send(far, shift("core", 1)).astype(jnp.float32)
        near_out = near.astype(jnp.bfloat16)
        first_share = total(near[0], [send(near_out[k], shift("zl", k)) for k in (1, 2, 3)])
        line_sum = total(second[0], came)
        line_out, first_share = lax.optimization_barrier((line_sum.astype(jnp.bfloat16), first_share))
        came = [send(line_out[2 * k : 2 * k + 2], shift_by_core(inner_axes, k)) for k in (2, 1, 3)]
        pair_sum = total(line_sum[:2], came)
        own, other = first_share - pair_sum[0], -pair_sum[1]
        if iteration == ITERS - 1:
            raw = own + send(other.astype(jnp.bfloat16), shift("zh", 1)).astype(jnp.float32)
            return block.astype(jnp.float32) + RATE * turn_back(raw)
        pieces = lax.optimization_barrier(jnp.stack([other, own]).astype(jnp.bfloat16))
        raw = jnp.stack([own, other]) + send(pieces, shift("zh", 1)).astype(jnp.float32)
        pair = (pair.astype(jnp.float32) + RATE * turn_back(raw)).astype(jnp.bfloat16)
        block = pair[0]


def solution(mesh):
    fine = Mesh(mesh.devices.reshape(SIZES), AXES)
    rows = P(AXES)
    return jax.shard_map(
        per_device, mesh=fine, in_specs=(rows,) * 6, out_specs=rows, check_vma=False
    )
```
